32 devices in a mesh: section: 2 (over core), tensor: 8 (over z, y), dp: 2 (over x).
Axes of the slice: x: 2, y: 2, z: 4, core: 2. Of those that a mesh axis runs over, the one named last changes fastest.
Arguments:
- inputs: bfloat16 [8, 1024, 1024], P('dp', 'tensor'), may hold values from -6 to 6
- cotangent: bfloat16 [8, 1024, 1024], P('dp', 'tensor'), may hold values from -6 to 6
- norm_gain: bfloat16 [2, 1024], P('section'), may hold values from 0.5 to 1.5
- w_zx: bfloat16 [2, 1024, 2, 2048], P('section', None, None, 'tensor'), may hold values from -0.25 to 0.25
- w_bc: bfloat16 [2, 1024, 256], P('section'), may hold values from -0.1875 to 0.1875
- w_dt: bfloat16 [2, 1024, 32], P('section', None, 'tensor'), may hold values from -0.1875 to 0.1875
- dt_bias: float32 [2, 32], P('section', 'tensor'), may hold values from -6 to -2
- a_log: float32 [2, 32], P('section', 'tensor'), may hold values from 0 to 2.5
- d_skip: float32 [2, 32], P('section', 'tensor'), may hold values from 0.5 to 1.5
- conv_x_w: bfloat16 [2, 4, 2048], P('section', None, 'tensor'), may hold values from -3 to 3
- conv_x_b: bfloat16 [2, 2048], P('section', 'tensor'), may hold values from -3 to 3
- conv_bc_w: bfloat16 [2, 4, 256], P('section'), may hold values from -3 to 3
- conv_bc_b: bfloat16 [2, 256], P('section'), may hold values from -3 to 3
- gate_gain: bfloat16 [2, 2048], P('section', 'tensor'), may hold values from 0.5 to 1.5
- w_out: bfloat16 [2, 2048, 1024], P('section', 'tensor'), may hold values from -0.125 to 0.125
Outputs:
- section_out: bfloat16 [2, 8, 1024, 1024], P('section', 'dp', 'tensor')
- section_grad: float32 [2, 8, 1024, 1024], P('section', 'dp', 'tensor')
- grad_norm_gain: float32 [2, 1024], P('section')
- grad_w_zx: float32 [2, 1024, 2, 2048], P('section', None, None, 'tensor')
- grad_w_bc: float32 [2, 1024, 256], P('section')
- grad_w_dt: float32 [2, 1024, 32], P('section', None, 'tensor')
- grad_dt_bias: float32 [2, 32], P('section', 'tensor')
- grad_a_log: float32 [2, 32], P('section', 'tensor')
- grad_d_skip: float32 [2, 32], P('section', 'tensor')
- grad_conv_x_w: float32 [2, 4, 2048], P('section', None, 'tensor')
- grad_conv_x_b: float32 [2, 2048], P('section', 'tensor')
- grad_conv_bc_w: float32 [2, 4, 256], P('section')
- grad_conv_bc_b: float32 [2, 256], P('section')
- grad_gate_gain: float32 [2, 2048], P('section', 'tensor')
- grad_w_out: float32 [2, 2048, 1024], P('section', 'tensor')
The draws below stay inside these ranges and needn't reach their ends.
All inputs are finite; a program needn't handle non-finite values.
Results may differ from the reference program's by a relative error of at most 0.019.
Values may be sent and summed in bfloat16 or wider, within the bound.
A program may use at most 256 MiB of HBM per device.

```python
import jax
import jax.numpy as jnp
from jax import lax

D = 1024
HEADS = 32
STATE = 128
KC = 4
BLOCK = 256
INNER = 2048
L = 1024
SEQ_MB = 2
SEQS = 8


def raised(drawn, rng, source, target, shards_of, factor):
    owner, partner = [(jnp.arange(drawn.shape[dim]) // (drawn.shape[dim] // shards_of)).reshape([-1 if axis == dim else 1 for axis in range(drawn.ndim)]) for dim in (source, target)]
    chosen = jax.random.permutation(rng, shards_of)[partner]
    strong = (owner == chosen) | (owner == (partner + shards_of // 2) % shards_of)
    return jnp.where(strong, factor * drawn, drawn)


def shard_levels(key, shape, split, smallest, high):
    loudness = 1.0
    for dim, blocks in split:
        heights = jax.random.uniform(jax.random.fold_in(jax.random.fold_in(key, 6), dim), (blocks,), jnp.float32, smallest / len(split), high / len(split))
        loudness = loudness * jnp.repeat(jnp.exp(heights), shape[dim] // blocks).reshape((-1,) + (1,) * (len(shape) - 1 - dim))
    return loudness


def normal_values(own_key, extent, width, bound, cuts=(), kind=jnp.bfloat16):
    gain = shard_levels(own_key, extent, cuts, -0.22, 0.18) if cuts else 1.0
    entries = jax.random.normal(own_key, extent, jnp.float32) * width * gain
    return jnp.minimum(jnp.maximum(entries, -bound), bound).astype(kind)


def heavy_noise(rng, extent, spread, bound, cuts, heavy, kind=jnp.bfloat16):
    entries = spread * jax.random.normal(rng, extent, jnp.float32)
    if cuts:
        entries = entries * shard_levels(rng, extent, cuts, -0.22, 0.18)
    return jnp.clip(raised(entries, jax.random.fold_in(rng, 3), *heavy), -bound, bound).astype(kind)


def setup_inputs(seed: int = 0) -> dict:
    key_of = jax.random.split(jax.random.key(seed), 16)
    inputs = normal_values(key_of[0], (SEQS, L, D), 1.0, 6.0, ((0, 2), (1, 8)))
    cotangent = normal_values(key_of[1], (SEQS, L, D), 1.0, 6.0, ((0, 2), (1, 8)))
    norm_gain = jnp.clip(1.0 + 0.1 * jax.random.normal(key_of[2], (2, D), jnp.float32), 0.5, 1.5).astype(jnp.bfloat16)
    w_zx = heavy_noise(key_of[3], (2, D, 2, INNER), D ** -0.5, 0.25, ((0, 2), (3, 8)), (3, 1, 8, 2.0))
    w_bc = normal_values(key_of[4], (2, D, 2 * STATE), D ** -0.5, 0.1875, ((0, 2),))
    w_dt = normal_values(key_of[5], (2, D, HEADS), D ** -0.5, 0.1875, ((0, 2), (2, 8)))
    dt_bias = jnp.clip(-6.0 + 4.0 * jax.random.uniform(key_of[6], (2, HEADS), jnp.float32) ** shard_levels(key_of[6], (2, HEADS), ((0, 2), (1, 8)), -0.2, 0.2), -6.0, -2.0)
    a_log = jnp.clip(2.5 * jax.random.uniform(key_of[7], (2, HEADS), jnp.float32) ** shard_levels(key_of[7], (2, HEADS), ((0, 2), (1, 8)), -0.2, 0.2), 0.0, 2.5)
    d_skip = jnp.clip(0.5 + 1.0 * jax.random.uniform(key_of[8], (2, HEADS), jnp.float32) ** shard_levels(key_of[8], (2, HEADS), ((0, 2), (1, 8)), -0.2, 0.2), 0.5, 1.5)
    conv_x_w = normal_values(key_of[9], (2, KC, INNER), KC ** -0.5, 3.0, ((0, 2), (2, 8)))
    conv_x_b = normal_values(key_of[10], (2, INNER), 0.5, 3.0, ((0, 2), (1, 8)))
    conv_bc_w = normal_values(key_of[11], (2, KC, 2 * STATE), KC ** -0.5, 3.0, ((0, 2),))
    conv_bc_b = normal_values(key_of[12], (2, 2 * STATE), 0.5, 3.0, ((0, 2),))
    gate_gain = jnp.clip(1.0 + 0.1 * jax.random.normal(key_of[13], (2, INNER), jnp.float32), 0.5, 1.5).astype(jnp.bfloat16)
    w_out = normal_values(key_of[14], (2, INNER, D), INNER ** -0.5, 0.125, ((0, 2), (1, 8)))
    return dict(inputs=inputs, cotangent=cotangent, norm_gain=norm_gain, w_zx=w_zx, w_bc=w_bc, w_dt=w_dt, dt_bias=dt_bias, a_log=a_log, d_skip=d_skip, conv_x_w=conv_x_w, conv_x_b=conv_x_b, conv_bc_w=conv_bc_w, conv_bc_b=conv_bc_b, gate_gain=gate_gain, w_out=w_out)


EPSILON = 1e-05
PRECISE = lax.Precision.HIGHEST

@jax.custom_vjp
def low(v):
    return lax.optimization_barrier(v.astype(jnp.bfloat16)).astype(jnp.float32)

@jax.custom_vjp
def low_back(v):
    return v

def low_keep(v):
    return (low(v), None)

def low_pass(kept, grad):
    return (grad,)

def back_keep(v):
    return (v, None)

def back_low(kept, grad):
    return (low(grad),)
low.defvjp(low_keep, low_pass)
low_back.defvjp(back_keep, back_low)

def causal_conv(values, weight, biases):
    taps = weight.shape[0]
    length = values.shape[1]
    padded = jnp.pad(values, ((0, 0), (taps - 1, 0), (0, 0)))
    summed = biases
    for offset in range(taps):
        summed = summed + padded[:, offset:offset + length, :] * weight[offset]
    return jax.nn.silu(summed)

def state_scan(x_heads, deltas, decay_rate, b_matrix, c_matrix):
    seq_count, length, head_count, head_size = x_heads.shape
    state_size = b_matrix.shape[-1]
    block_count = length // BLOCK
    x_heads = x_heads.reshape(seq_count, block_count, BLOCK, head_count, head_size)
    deltas = deltas.reshape(seq_count, block_count, BLOCK, head_count)
    b_matrix = b_matrix.reshape(seq_count, block_count, BLOCK, state_size)
    c_matrix = c_matrix.reshape(seq_count, block_count, BLOCK, state_size)
    cumulative = jnp.cumsum(deltas * decay_rate, axis=2)
    differences = cumulative[:, :, :, None, :] - cumulative[:, :, None, :, :]
    causal = (jnp.arange(BLOCK)[:, None] >= jnp.arange(BLOCK)[None, :])[None, None, :, :, None]
    decays = jnp.where(causal, jnp.exp(jnp.minimum(differences, 0.0)), 0.0)
    affinity = jnp.einsum('nclk,ncmk->nclm', c_matrix, b_matrix, precision=PRECISE)
    weights = affinity[..., None] * decays * deltas[:, :, None, :, :]
    within = jnp.einsum('nclmh,ncmhp->nclhp', weights, x_heads, precision=PRECISE)
    closing = cumulative[:, :, -1, :]
    scaled = jnp.exp(closing[:, :, None, :] - cumulative) * deltas
    states = jnp.einsum('ncmh,ncmk,ncmhp->nchkp', scaled, b_matrix, x_heads, precision=PRECISE)

    def carry_step(running, pieces):
        block_state, fall_rate = pieces
        return (running * jnp.exp(fall_rate)[:, :, None, None] + block_state, running)
    initial = jnp.zeros((seq_count, head_count, state_size, head_size), x_heads.dtype)
    _, entering = lax.scan(carry_step, initial, (jnp.moveaxis(states, 1, 0), jnp.moveaxis(closing, 1, 0)))
    entering = jnp.moveaxis(entering, 0, 1)
    carried = jnp.einsum('nclk,nchkp->nclhp', c_matrix, entering, precision=PRECISE) * jnp.exp(cumulative)[..., None]
    return (within + carried).reshape(seq_count, length, head_count, head_size)

def mixer_part(z_and_x, b_and_c, dt_raw, conv_x_w, conv_x_b, conv_bc_w, conv_bc_b, dt_bias, a_log, d_skip, seq_count):
    row_count = z_and_x.shape[0]
    inner_size = z_and_x.shape[1] // 2
    head_count = dt_raw.shape[1]
    head_size = inner_size // head_count
    state_size = b_and_c.shape[1] // 2
    length = row_count // seq_count
    gate_in = z_and_x[:, :inner_size]
    x_conv = causal_conv(z_and_x[:, inner_size:].reshape(seq_count, length, inner_size), conv_x_w, conv_x_b)
    bc_conv = causal_conv(b_and_c.reshape(seq_count, length, 2 * state_size), conv_bc_w, conv_bc_b)
    deltas = jax.nn.softplus(dt_raw + dt_bias).reshape(seq_count, length, head_count)
    decay_rate = -jnp.exp(a_log)
    x_heads = x_conv.reshape(seq_count, length, head_count, head_size)
    scanned = state_scan(x_heads, deltas, decay_rate, bc_conv[..., :state_size], bc_conv[..., state_size:])
    scanned = scanned + d_skip[:, None] * x_heads
    return scanned.reshape(row_count, inner_size) * jax.nn.silu(gate_in)

def mamba_layer(hidden, params, seq_count):
    norm_gain, w_zx, w_bc, w_dt, dt_bias, a_log, d_skip, conv_x_w, conv_x_b, conv_bc_w, conv_bc_b, gate_gain, w_out = params
    model_width = hidden.shape[1]
    scale_in = lax.rsqrt(lax.optimization_barrier(jnp.mean(hidden * hidden, axis=-1, keepdims=True)) + EPSILON)
    normed = low(hidden * scale_in * norm_gain)
    z_and_x = low_back(jnp.dot(normed, w_zx.reshape(model_width, -1), precision=PRECISE, preferred_element_type=jnp.float32))
    b_and_c = low_back(jnp.dot(normed, w_bc, precision=PRECISE, preferred_element_type=jnp.float32))
    dt_raw = low_back(jnp.dot(normed, w_dt, precision=PRECISE, preferred_element_type=jnp.float32))
    gated = mixer_part(z_and_x, b_and_c, dt_raw, conv_x_w, conv_x_b, conv_bc_w, conv_bc_b, dt_bias, a_log, d_skip, seq_count)
    scale_gate = lax.rsqrt(lax.optimization_barrier(jnp.mean(gated * gated, axis=-1, keepdims=True)) + EPSILON)
    mixed = low(gated * scale_gate * gate_gain)
    return hidden + jnp.dot(mixed, w_out, precision=PRECISE, preferred_element_type=jnp.float32)

def reference(inputs, cotangent, norm_gain, w_zx, w_bc, w_dt, dt_bias, a_log, d_skip, conv_x_w, conv_x_b, conv_bc_w, conv_bc_b, gate_gain, w_out):
    weights = tuple((argument.astype(jnp.float32) for argument in (norm_gain, w_zx, w_bc, w_dt, dt_bias, a_log, d_skip, conv_x_w, conv_x_b, conv_bc_w, conv_bc_b, gate_gain, w_out)))
    first_set = tuple((argument[0] for argument in weights))
    second_set = tuple((argument[1] for argument in weights))
    group_count = SEQS // SEQ_MB
    row_count = SEQ_MB * L
    hidden_in = inputs.astype(jnp.float32).reshape(group_count, row_count, D)
    seed_in = cotangent.astype(jnp.float32).reshape(group_count, row_count, D)

    def forward(hidden, probe_term, lower_set, upper_set):
        first_out = mamba_layer(hidden, lower_set, SEQ_MB)
        second_in = low_back(low(first_out)) + probe_term
        return (first_out, mamba_layer(second_in, upper_set, SEQ_MB))

    def sequence_group(totals, batch_pair):
        hidden, seed_grad = batch_pair
        outputs, pullback = jax.vjp(forward, hidden, jnp.zeros_like(hidden), first_set, second_set)
        grad_in, grad_mid, grad_lower, grad_upper = pullback((jnp.zeros_like(outputs[0]), seed_grad))
        totals = jax.tree.map(jnp.add, totals, (grad_lower, grad_upper))
        return (totals, (outputs[0].astype(jnp.bfloat16), outputs[1].astype(jnp.bfloat16), grad_in, grad_mid))
    zero_grads = jax.tree.map(jnp.zeros_like, (first_set, second_set))
    totals, (lower_out, upper_out, grad_in, grad_mid) = lax.scan(sequence_group, zero_grads, (hidden_in, seed_in))
    section_out = jnp.stack([lower_out.reshape(SEQS, L, D), upper_out.reshape(SEQS, L, D)])
    section_grad = jnp.stack([grad_in.reshape(SEQS, L, D), grad_mid.reshape(SEQS, L, D)])
    grads = tuple((jnp.stack([lower_grad, upper_grad]) for lower_grad, upper_grad in zip(totals[0], totals[1])))
    return (section_out, section_grad, grads[0], grads[1], grads[2], grads[3], grads[4], grads[5], grads[6], grads[7], grads[8], grads[9], grads[10], grads[11], grads[12])
```

```python
import functools

import jax
import jax.numpy as jnp
from jax import lax
from jax.experimental import pallas as pl
from jax.experimental.pallas import tpu as pltpu
from jax.sharding import PartitionSpec as P

BLOCK = 256
HEAD = 64
DTW = 128
EPSILON = 1e-05
F32 = jnp.float32
BF16 = jnp.bfloat16
VMEM_BYTES = 48 * 1024 * 1024

DIMS = {"nn": ((1,), (0,)), "nt": ((1,), (1,)), "tn": ((0,), (0,))}


def plain_dot(a, b, mode, exact):
    if exact:
        return lax.dot_general(
            a, b, (DIMS[mode], ((), ())), precision=lax.Precision.HIGHEST, preferred_element_type=F32
        )
    return lax.dot_general(
        a.astype(BF16), b.astype(BF16), (DIMS[mode], ((), ())), preferred_element_type=F32
    )


def make_dot(mode, exact):
    @jax.custom_vjp
    def dot(a, b):
        return plain_dot(a, b, mode, exact)

    def keep(a, b):
        return plain_dot(a, b, mode, exact), (a, b)

    def back(kept, g):
        a, b = kept
        if mode == "nn":
            return plain_dot(g, b, "nt", exact), plain_dot(a, g, "tn", exact)
        if mode == "nt":
            return plain_dot(g, b, "nn", exact), plain_dot(g, a, "tn", exact)
        return plain_dot(b, g, "nt", exact), plain_dot(a, g, "nn", exact)

    dot.defvjp(keep, back)
    return dot


dot_nn = make_dot("nn", False)
dot_nt = make_dot("nt", False)
dot_tn = make_dot("tn", False)
exact_nn = make_dot("nn", True)


@jax.custom_vjp
def softplus(v):
    return jnp.maximum(v, 0.0) + jnp.log1p(jnp.exp(-jnp.abs(v)))


softplus.defvjp(lambda v: (softplus(v), v), lambda v, g: (g * lax.logistic(v),))


@functools.partial(jax.custom_vjp, nondiff_argnums=(2,))
def delayed(halo, values, distance):
    joined = jnp.concatenate([halo, values], axis=0)
    if distance:
        joined = pltpu.roll(joined, distance, 0)
    return joined[8:]


def delayed_keep(halo, values, distance):
    return delayed(halo, values, distance), None


def delayed_back(distance, kept, g):
    joined = jnp.concatenate([jnp.zeros((8, g.shape[1]), g.dtype), g], axis=0)
    if distance:
        joined = pltpu.roll(joined, joined.shape[0] - distance, 0)
    return joined[:8], joined[8:]


delayed.defvjp(delayed_keep, delayed_back)


def conv_silu(halo, values, taps, bias):
    count = len(taps)
    summed = bias + values * taps[count - 1]
    for k in range(count - 1):
        summed = summed + delayed(halo, values, count - 1 - k) * taps[k]
    return summed * lax.logistic(summed)


def block_mixer(z, x, b, c, dt, hx, hb, hc, state, xt, bt, ct, xb, bb, cb, dt_bias, a_log, skip):
    rows, inner = x.shape
    heads = inner // HEAD
    xc = conv_silu(hx, x, xt, xb)
    bm = conv_silu(hb, b, bt, bb)
    cm = conv_silu(hc, c, ct, cb)
    delta = softplus(dt + dt_bias)
    falls = delta * (-jnp.exp(a_log))
    row_id = lax.broadcasted_iota(jnp.int32, (rows, rows), 0)
    col_id = lax.broadcasted_iota(jnp.int32, (rows, rows), 1)
    causal = row_id >= col_id
    cum = exact_nn(jnp.where(causal, 1.0, 0.0).astype(F32), falls)
    closing = jnp.sum(falls, axis=0, keepdims=True)
    spread_row = lax.broadcasted_iota(jnp.int32, (DTW, inner), 0)
    spread_col = lax.broadcasted_iota(jnp.int32, (DTW, inner), 1)
    spread = jnp.where(
        (spread_col >= spread_row * HEAD) & (spread_col < (spread_row + 1) * HEAD), 1.0, 0.0
    ).astype(F32)
    xd = xc * exact_nn(delta, spread)
    cum_t = jnp.transpose(cum)
    affinity = dot_nt(cm, bm)
    lane = lax.broadcasted_iota(jnp.int32, (rows, DTW), 1)
    sub = lax.broadcasted_iota(jnp.int32, (DTW, rows), 0)
    chan = lax.broadcasted_iota(jnp.int32, (rows, inner), 1)
    y = dot_nn(cm, state) * exact_nn(jnp.exp(cum), spread) + skip * xc
    for h in range(heads):
        col = jnp.sum(jnp.where(lane == h, cum, 0.0), axis=1, keepdims=True)
        row = jnp.sum(jnp.where(sub == h, cum_t, 0.0), axis=0, keepdims=True)
        decay = jnp.exp(jnp.where(causal, col - row, -1e30))
        own = (chan >= h * HEAD) & (chan < (h + 1) * HEAD)
        y = y + dot_nn(affinity * decay, jnp.where(own, xd, 0.0))
    leaving = jnp.broadcast_to(jnp.exp(closing) * 0.125, (8, DTW))
    kept = jnp.sum(exact_nn(leaving, spread), axis=0, keepdims=True)
    scaled = xd * exact_nn(jnp.exp(closing - cum), spread)
    state_out = state * kept + dot_tn(bm, scaled)
    return y * (z * lax.logistic(z)), state_out


def block_args(proj, halo, live, par_x, par_bc, par_dt, inner):
    z = proj[:, :inner]
    x = proj[:, inner : 2 * inner]
    at = 2 * inner
    b = proj[:, at : at + 128]
    c = proj[:, at + 128 : at + 256]
    dt = proj[:, at + 256 : at + 256 + DTW]
    hx = halo[:, inner : 2 * inner] * live
    hb = halo[:, at : at + 128] * live
    hc = halo[:, at + 128 : at + 256] * live
    xt = [par_x[k : k + 1, :] for k in range(4)]
    bt = [par_bc[k : k + 1, :128] for k in range(4)]
    ct = [par_bc[k : k + 1, 128:] for k in range(4)]
    tail = (
        xt, bt, ct,
        par_x[4:5, :], par_bc[4:5, :128], par_bc[4:5, 128:],
        par_dt[0:1, :], par_dt[1:2, :], par_x[5:6, :],
    )
    return (z, x, b, c, dt, hx, hb, hc), tail


def forward_kernel(proj, halo, par_x, par_bc, par_dt, g_out, state_out, state):
    inner = par_x.shape[1]
    step = pl.program_id(0)

    @pl.when(step == 0)
    def _():
        state[...] = jnp.zeros_like(state)

    live = jnp.where(step > 0, 1.0, 0.0).astype(F32)
    head, tail = block_args(proj, halo, live, par_x, par_bc, par_dt, inner)
    entering = state[...]
    state_out[0] = entering
    g, leaving = block_mixer(*head, entering, *tail)
    g_out[...] = g
    state[...] = leaving


def backward_kernel(
    proj, halo, entering, dg, par_x, par_bc, par_dt, dproj, gx, gbc, gdt, dstate, dhalo
):
    inner = par_x.shape[1]
    step = pl.program_id(0)
    last = pl.num_programs(0) - 1

    @pl.when(step == 0)
    def _():
        dstate[...] = jnp.zeros_like(dstate)
        dhalo[...] = jnp.zeros_like(dhalo)
        gx[...] = jnp.zeros_like(gx)
        gbc[...] = jnp.zeros_like(gbc)
        gdt[...] = jnp.zeros_like(gdt)

    live = jnp.where(step < last, 1.0, 0.0).astype(F32)
    head, tail = block_args(proj, halo, live, par_x, par_bc, par_dt, inner)
    _, pull = jax.vjp(block_mixer, *head, entering[0], *tail)
    (dz, dx, db, dc, ddt, dhx, dhb, dhc, dst, dxt, dbt, dct, dxb, dbb, dcb, dtb, dal, dsk) = pull(
        (dg[...], dstate[...])
    )
    dstate[...] = dst

    def joined(values, low, high):
        end = values.shape[0] - 8
        return jnp.concatenate([values[:end], values[end:] + dhalo[:, low:high]], axis=0).astype(
            BF16
        )

    at = 2 * inner
    dproj[:, :inner] = dz.astype(BF16)
    dproj[:, inner:at] = joined(dx, 0, inner)
    dproj[:, at : at + 128] = joined(db, inner, inner + 128)
    dproj[:, at + 128 : at + 256] = joined(dc, inner + 128, inner + 256)
    dproj[:, at + 256 : at + 256 + DTW] = ddt.astype(BF16)
    dhalo[:, :inner] = dhx
    dhalo[:, inner : inner + 128] = dhb
    dhalo[:, inner + 128 :] = dhc
    for k in range(4):
        gx[k : k + 1, :] += dxt[k]
        gbc[k : k + 1, :128] += dbt[k]
        gbc[k : k + 1, 128:] += dct[k]
    gx[4:5, :] += dxb
    gbc[4:5, :128] += dbb
    gbc[4:5, 128:] += dcb
    gx[5:6, :] += dsk
    gdt[0:1, :] += dtb
    gdt[1:2, :] += dal


def whole(shape):
    return pl.BlockSpec(shape, lambda i: (0,) * len(shape))


def run_forward(proj, par_x, par_bc, par_dt):
    rows, width = proj.shape
    inner = par_x.shape[1]
    blocks = rows // BLOCK
    lead = BLOCK // 8
    return pl.pallas_call(
        forward_kernel,
        grid=(blocks,),
        in_specs=[
            pl.BlockSpec((BLOCK, width), lambda i: (i, 0)),
            pl.BlockSpec((8, width), lambda i: (jnp.maximum(i * lead - 1, 0), 0)),
            whole(par_x.shape),
            whole(par_bc.shape),
            whole(par_dt.shape),
        ],
        out_specs=[
            pl.BlockSpec((BLOCK, inner), lambda i: (i, 0)),
            pl.BlockSpec((1, 128, inner), lambda i: (i, 0, 0)),
        ],
        out_shape=[
            jax.ShapeDtypeStruct((rows, inner), F32),
            jax.ShapeDtypeStruct((blocks, 128, inner), F32),
        ],
        scratch_shapes=[pltpu.VMEM((128, inner), F32)],
        compiler_params=pltpu.CompilerParams(vmem_limit_bytes=VMEM_BYTES),
        cost_estimate=pl.CostEstimate(
            flops=rows * inner * 20000, bytes_accessed=rows * width * 8, transcendentals=rows * 1024
        ),
    )(proj, proj, par_x, par_bc, par_dt)


def run_backward(proj, entering, dg, par_x, par_bc, par_dt):
    rows, width = proj.shape
    inner = par_x.shape[1]
    blocks = rows // BLOCK
    lead = BLOCK // 8
    top = blocks - 1
    return pl.pallas_call(
        backward_kernel,
        grid=(blocks,),
        in_specs=[
            pl.BlockSpec((BLOCK, width), lambda i: (top - i, 0)),
            pl.BlockSpec((8, width), lambda i: (jnp.maximum((top - i) * lead - 1, 0), 0)),
            pl.BlockSpec((1, 128, inner), lambda i: (top - i, 0, 0)),
            pl.BlockSpec((BLOCK, inner), lambda i: (top - i, 0)),
            whole(par_x.shape),
            whole(par_bc.shape),
            whole(par_dt.shape),
        ],
        out_specs=[
            pl.BlockSpec((BLOCK, width), lambda i: (top - i, 0)),
            whole(par_x.shape),
            whole(par_bc.shape),
            whole(par_dt.shape),
        ],
        out_shape=[
            jax.ShapeDtypeStruct((rows, width), BF16),
            jax.ShapeDtypeStruct(par_x.shape, F32),
            jax.ShapeDtypeStruct(par_bc.shape, F32),
            jax.ShapeDtypeStruct(par_dt.shape, F32),
        ],
        scratch_shapes=[pltpu.VMEM((128, inner), F32), pltpu.VMEM((8, inner + 256), F32)],
        compiler_params=pltpu.CompilerParams(vmem_limit_bytes=VMEM_BYTES),
        cost_estimate=pl.CostEstimate(
            flops=rows * inner * 60000, bytes_accessed=rows * width * 8, transcendentals=rows * 1024
        ),
    )(proj, proj, entering, dg, par_x, par_bc, par_dt)


def rows8(*members):
    stacked = jnp.concatenate([m.astype(F32) for m in members], axis=0)
    return jnp.pad(stacked, ((0, 8 - stacked.shape[0]), (0, 0)))


def body(
    inputs,
    cotangent,
    norm_gain,
    w_zx,
    w_bc,
    w_dt,
    dt_bias,
    a_log,
    d_skip,
    conv_x_w,
    conv_x_b,
    conv_bc_w,
    conv_bc_b,
    gate_gain,
    w_out,
):
    section_count = lax.axis_size("section")
    here = lax.axis_index("section")
    tensor_count = lax.axis_size("tensor")
    tensor_id = lax.axis_index("tensor")
    dp_count = lax.axis_size("dp")
    seq_dev, rows_own, width = inputs.shape
    length = rows_own * tensor_count
    inner = w_zx.shape[3]
    heads = w_dt.shape[2]
    mine = seq_dev // section_count
    total_inner = inner * tensor_count
    first = here == 0
    swap = [(0, 1), (1, 0)]

    def other(value):
        return lax.ppermute(value, "section", swap)

    def both(own):
        got = other(own)
        return jnp.where(first, own, got), jnp.where(first, got, own)

    w_all_own = jnp.concatenate(
        [
            w_zx[0].reshape(width, 2 * inner),
            w_bc[0],
            jnp.pad(w_dt[0], ((0, 0), (0, DTW - heads))),
        ],
        axis=1,
    )
    small_own = jnp.concatenate(
        [
            rows8(conv_x_w[0], conv_x_b, jnp.repeat(d_skip, HEAD, axis=1), gate_gain),
            rows8(conv_bc_w[0], conv_bc_b),
            rows8(*[jnp.pad(m, ((0, 0), (0, DTW - heads))) for m in (dt_bias, a_log)]),
            rows8(norm_gain),
        ],
        axis=1,
    )
    smalls = both(small_own)
    w_alls = both(w_all_own)
    w_outs = both(w_out[0])
    par = []
    for small in smalls:
        at = inner + 256
        par.append(
            dict(
                x=small[:, :inner],
                bc=small[:, inner:at],
                dt=small[:, at : at + DTW],
                gain=small[0:1, at + DTW :],
                gate=small[6:7, :inner],
            )
        )

    rows_in = lax.dynamic_slice_in_dim(inputs, here * mine, mine, 0)
    seeds = lax.dynamic_slice_in_dim(cotangent, here * mine, mine, 0)

    hidden_low = [rows_in[s] for s in range(mine)]
    kept = []
    outs = []
    for layer in range(2):
        p = par[layer]
        layer_kept = []
        layer_out = []
        for s in range(mine):
            hidden = hidden_low[s].astype(F32)
            scale_in = lax.rsqrt(jnp.mean(hidden * hidden, axis=-1, keepdims=True) + EPSILON)
            normed_own = (hidden * scale_in * p["gain"]).astype(BF16)
            normed = lax.all_gather(normed_own, "tensor", axis=0, tiled=True)
            proj = jnp.dot(normed, w_alls[layer], preferred_element_type=F32)
            gated, entering = run_forward(proj, p["x"], p["bc"], p["dt"])
            squares = lax.psum(jnp.sum(gated * gated, axis=-1), "tensor")
            partial = jnp.dot(
                (gated * p["gate"]).astype(BF16), w_outs[layer], preferred_element_type=F32
            ).astype(BF16)
            raw = lax.psum_scatter(partial, "tensor", scatter_dimension=0, tiled=True).astype(F32)
            scale_gate = lax.rsqrt(squares / total_inner + EPSILON)
            scale_own = lax.dynamic_slice_in_dim(scale_gate, tensor_id * rows_own, rows_own, 0)
            out_low = (hidden + scale_own[:, None] * raw).astype(BF16)
            layer_out.append(out_low)
            layer_kept.append((hidden, scale_in, normed, proj, gated, entering, raw, scale_gate))
        hidden_low = layer_out
        kept.append(layer_kept)
        outs.append(jnp.stack(layer_out))

    grad_low = [seeds[s] for s in range(mine)]
    grads = [None, None]
    grad_rows = [None, None]
    for layer in (1, 0):
        p = par[layer]
        layer_grad = []
        total = None
        for s in range(mine):
            hidden, scale_in, normed, proj, gated, entering, raw, scale_gate = kept[layer][s]
            own = grad_low[s].astype(F32)
            dot = lax.all_gather(jnp.sum(own * raw, axis=-1), "tensor", axis=0, tiled=True)
            full = lax.all_gather(grad_low[s], "tensor", axis=0, tiled=True)
            q = scale_gate[:, None]
            d_mixed = plain_dot(full, w_outs[layer], "nt", False)
            mixed = (gated * q * p["gate"]).astype(BF16)
            g_gate = jnp.sum(d_mixed * gated * q, axis=0)
            d_gated = q * p["gate"] * d_mixed - gated * (
                q * q * q * (dot[:, None] / total_inner)
            )
            d_proj, g_x, g_bc, g_dt = run_backward(
                proj, entering, d_gated, p["x"], p["bc"], p["dt"]
            )
            d_normed = plain_dot(d_proj, w_alls[layer], "nt", False).astype(BF16)
            d_in = lax.psum_scatter(
                d_normed, "tensor", scatter_dimension=0, tiled=True
            ).astype(F32)
            g_gain = jnp.sum(d_in * hidden * scale_in, axis=0)
            inner_dot = jnp.sum(hidden * p["gain"] * d_in, axis=-1, keepdims=True)
            d_hidden = (
                own
                + scale_in * p["gain"] * d_in
                - hidden * (scale_in * scale_in * scale_in * (inner_dot / width))
            )
            layer_grad.append(d_hidden)
            g_all = plain_dot(normed, d_proj, "tn", False)
            g_out = plain_dot(mixed, full, "tn", False)
            members = (g_all, g_out, g_x, g_bc, g_dt, g_gate, g_gain)
            total = members if total is None else tuple(a + b for a, b in zip(total, members))
        grad_rows[layer] = jnp.stack(layer_grad)
        grad_low = [g.astype(BF16) for g in layer_grad]
        grads[layer] = total

    def settle(pair, dtype):
        keep = jnp.where(first, pair[0], pair[1])
        send = jnp.where(first, pair[1], pair[0]).astype(dtype)
        return keep + other(send).astype(F32)

    def over_dp(value, dtype):
        low = value.astype(dtype)
        if dp_count == 2:
            return low.astype(F32) + lax.ppermute(low, "dp", swap).astype(F32)
        return lax.psum(low, "dp").astype(F32)

    g_all = settle([grads[0][0], grads[1][0]], BF16)
    g_out = settle([grads[0][1], grads[1][1]], BF16)

    def small_pack(g):
        x = jnp.concatenate([g[2][:6], g[5][None], jnp.zeros((1, inner), F32)], axis=0)
        shared = jnp.concatenate([g[3], jnp.broadcast_to(g[6][None] * 0.125, (8, width))], axis=1)
        return jnp.concatenate([x, g[4], shared], axis=1)

    small = settle([small_pack(grads[0]), small_pack(grads[1])], F32)
    at = inner + DTW
    shared_small, g_bc = lax.psum(
        (small[:, at:], g_all[:, 2 * inner : 2 * inner + 256]), ("tensor", "dp")
    )
    sharded = over_dp(small[:, :at], F32)
    g_zx = over_dp(g_all[:, : 2 * inner], BF16)
    g_dt = over_dp(g_all[:, 2 * inner + 256 :], BF16)[:, :heads]
    g_out = over_dp(g_out, BF16)

    def exchanged(pair):
        keep = jnp.where(first, pair[0], pair[1])
        got = other(jnp.where(first, pair[1], pair[0]))
        return jnp.concatenate(
            [jnp.where(first, keep, got), jnp.where(first, got, keep)], axis=0
        )[None]

    return (
        exchanged(outs),
        exchanged(grad_rows),
        jnp.sum(shared_small[:, 256:], axis=0)[None],
        g_zx.reshape(1, width, 2, inner),
        g_bc[None],
        g_dt[None],
        sharded[0:1, inner : inner + heads],
        sharded[1:2, inner : inner + heads],
        jnp.sum(sharded[5, :inner].reshape(heads, HEAD), axis=1)[None],
        sharded[None, 0:4, :inner],
        sharded[4:5, :inner],
        shared_small[None, 0:4, :256],
        shared_small[4:5, :256],
        sharded[6:7, :inner],
        g_out[None],
    )


def solution(mesh):
    specs_in = (
        P("dp", "tensor", None),
        P("dp", "tensor", None),
        P("section", None),
        P("section", None, None, "tensor"),
        P("section", None, None),
        P("section", None, "tensor"),
        P("section", "tensor"),
        P("section", "tensor"),
        P("section", "tensor"),
        P("section", None, "tensor"),
        P("section", "tensor"),
        P("section", None, None),
        P("section", None),
        P("section", "tensor"),
        P("section", "tensor", None),
    )
    specs_out = (
        P("section", "dp", "tensor", None),
        P("section", "dp", "tensor", None),
        *specs_in[2:],
    )
    return jax.shard_map(
        body, mesh=mesh, in_specs=specs_in, out_specs=specs_out, check_vma=False
    )
```
